32 devices in a mesh: row: 8 (over z, x), col: 4 (over y, core).
Axes of the slice: x: 2, y: 2, z: 4, core: 2. Of those that a mesh axis runs over, the one named last changes fastest.
Arguments:
- vectors: float32 [65536, 2048], P('row', 'col'), may hold values from -6 to 6
- reflectors: float32 [65536, 256], P('row'), may hold values from -0.09375 to 0.09375
- panel_factor: float32 [256, 256], replicated, as said below
- station_rows: int32 [512, 4], replicated, may hold values from 0 to 65535
- station_weights: float32 [512, 4], replicated, may hold values from -3 to 3
- event_rows: int32 [8, 4], replicated, may hold values from 0 to 65535
- event_weights: float32 [8, 4], replicated, may hold values from -3 to 3
- mode_freq: float32 [2048], P('col'), may hold values from 0.05 to 1.5
- mode_damp: float32 [2048], P('col'), may hold values from 0.0001 to 0.005
Outputs:
- rotated: float32 [65536, 2048], P('row', 'col')
- seismograms: float32 [8, 512, 1024], P(None, 'row', 'col')
The draws below stay inside these ranges and needn't reach their ends.
Inputs may be any that keep to these rules, and one draw needn't show every extreme that they name: panel_factor is upper triangular with a positive diagonal.
All inputs are finite; a program needn't handle non-finite values.
Results may differ from the reference program's by a relative error of at most 0.0003.
Values sent between devices are 32-bit elements; how exact they have to be, the bound alone decides.
A program may use at most 128 MiB of HBM per device.

```python
import math
import jax
import jax.numpy as jnp
from jax import lax

NMAT = 65536
NMODE = 2048
PW = 256
COMP = 512
EV = 8
TAPS = 4
NT = 1024


def draw_panel_factor(key, part):
    key_off, key_diag = jax.random.split(jax.random.fold_in(key, 17))
    upper = jax.random.normal(key_off, (PW, PW), jnp.float32) * (0.5 / PW ** 0.5)
    diag_vals = jax.random.uniform(key_diag, (PW,), jnp.float32, 1.0, 2.0)
    upper = jnp.triu(upper, 1)
    return upper + jnp.diag(diag_vals)


def set_ends(result, stream_key, least, largest):
    place = [jax.random.randint(jax.random.fold_in(stream_key, axis), (), 0, length) for axis, length in enumerate(result.shape)]
    widest = result.shape.index(max(result.shape))
    beside = place[:widest] + [(place[widest] + 1) % result.shape[widest]] + place[widest + 1:]
    return result.at[tuple(place)].set(least).at[tuple(beside)].set(largest)


def levels(own_key, shape, shards, least, high):
    gain, own = 1.0, jax.random.fold_in(own_key, 6)
    for position, blocks in shards:
        steps = jnp.exp(jax.random.uniform(jax.random.fold_in(own, position), (blocks,), jnp.float32, least / len(shards), high / len(shards)))
        gain = gain * jnp.repeat(steps, shape[position] // blocks).reshape([-1 if axis == position else 1 for axis in range(len(shape))])
    return gain


def bell_draw(key, dims, width, limit, cuts=(), kind=jnp.bfloat16):
    result = width * jax.random.normal(key, dims, jnp.float32)
    if cuts:
        result = result * levels(key, dims, cuts, -0.22, 0.18)
    return jnp.clip(result, -limit, limit).astype(kind)


def setup_inputs(seed: int = 0) -> dict:
    seeds = jax.random.split(jax.random.key(seed), 10)
    vectors = bell_draw(seeds[0], (NMAT, NMODE), 1.0, 6.0, ((0, 8), (1, 4)), jnp.float32)
    reflectors = bell_draw(seeds[1], (NMAT, PW), (4.0 / NMAT ** 0.5), 0.09375, ((0, 8),), jnp.float32)
    panel_factor = draw_panel_factor(jax.random.fold_in(seeds[9], 71), 0)
    station_rows = set_ends(jax.random.randint(seeds[3], (COMP, TAPS), 0, NMAT), jax.random.fold_in(seeds[3], 1), 0, NMAT - 1).astype(jnp.int32)
    station_weights = bell_draw(seeds[4], (COMP, TAPS), 0.5, 3.0, (), jnp.float32)
    event_rows = set_ends(jax.random.randint(seeds[5], (EV, TAPS), 0, NMAT), jax.random.fold_in(seeds[5], 1), 0, NMAT - 1).astype(jnp.int32)
    event_weights = bell_draw(seeds[6], (EV, TAPS), 0.5, 3.0, (), jnp.float32)
    mode_freq = jnp.clip(jnp.exp(math.log(1.5) - 3.4011974 * jax.random.uniform(seeds[7], (NMODE,), jnp.float32) ** levels(seeds[7], (NMODE,), ((0, 4),), -0.2, 0.2)), 0.05, 1.5)
    mode_damp = jnp.clip(jnp.exp(math.log(0.005) - 3.912023 * jax.random.uniform(seeds[8], (NMODE,), jnp.float32) ** levels(seeds[8], (NMODE,), ((0, 4),), -0.2, 0.2)), 0.0001, 0.005)
    return {"vectors": vectors, "reflectors": reflectors, "panel_factor": panel_factor, "station_rows": station_rows, "station_weights": station_weights, "event_rows": event_rows, "event_weights": event_weights, "mode_freq": mode_freq, "mode_damp": mode_damp}


def reference(vectors, reflectors, panel_factor, station_rows, station_weights, event_rows, event_weights, mode_freq, mode_damp):
    high = lax.Precision.HIGHEST
    panel = jnp.dot(reflectors.T, vectors, precision=high, preferred_element_type=jnp.float32)
    folded = jnp.dot(panel_factor, panel, precision=high, preferred_element_type=jnp.float32)
    rotated = vectors - jnp.dot(reflectors, folded, precision=high, preferred_element_type=jnp.float32)
    receivers = lax.optimization_barrier(jnp.sum(rotated[station_rows] * station_weights[:, :, None], axis=1))
    sources = lax.optimization_barrier(jnp.sum(rotated[event_rows] * event_weights[:, :, None], axis=1))
    times = jnp.arange(NT).astype(jnp.float32)
    basis = jnp.exp(-mode_damp[:, None] * times[None, :]) * jnp.cos(mode_freq[:, None] * times[None, :])
    amplitude = (sources[:, None, :] * receivers[None, :, :]).reshape(EV * COMP, NMODE)
    summed = jnp.dot(amplitude, basis, precision=high, preferred_element_type=jnp.float32)
    seismograms = summed.reshape(EV, COMP, NT) * (1.0 / math_sqrt(NMODE))
    return (rotated, seismograms)

def math_sqrt(value):
    return float(value) ** 0.5
```

```python
import functools
import math

import jax
import jax.numpy as jnp
import numpy as np
from jax import lax
from jax.experimental import pallas as pl
from jax.experimental.pallas import tpu as pltpu
from jax.sharding import PartitionSpec as P

MESH = pl.DeviceIdType.MESH
F32 = jnp.float32
BF16 = jnp.bfloat16
GROUP = 4
PARTS = 2

TURN_A = 6.28125
TURN_B = float(np.round((2 * math.pi - TURN_A) * 2**20) / 2**20)
TURN_C = 2 * math.pi - TURN_A - TURN_B


def cos_series():
    square = np.linspace(0.0, (1.01 * math.pi) ** 2, 4001)
    fit = np.polynomial.Chebyshev.fit(square, np.cos(np.sqrt(square)), 7)
    return [float(c) for c in fit.convert(kind=np.polynomial.Polynomial).coef]


COS = cos_series()


def cosine(x):
    turns = jnp.floor(x * (0.5 / math.pi) + 0.5)
    rest = ((x - turns * TURN_A) - turns * TURN_B) - turns * TURN_C
    square = rest * rest
    total = jnp.full_like(square, COS[-1])
    for coefficient in COS[-2::-1]:
        total = total * square + coefficient
    return total


def split(x):
    high = x.astype(BF16)
    return high, (x - high.astype(F32)).astype(BF16)


def dot3(a, b, over):
    dims = (((over[0],), (over[1],)), ((), ()))
    dot = functools.partial(lax.dot_general, dimension_numbers=dims, preferred_element_type=F32)
    return dot(a[0], b[0]) + (dot(a[0], b[1]) + dot(a[1], b[0]))


def panel_kernel(
    sizes,
    taps_ref,
    weights_ref,
    vec_hbm,
    refl_hbm,
    factor_ref,
    modes_ref,
    high_ref,
    low_ref,
    seis_ref,
    vec,
    refl,
    part,
    part_got,
    mine,
    mine_got,
    panel,
    whole,
    picked,
    picked_refl,
    sums,
    sums_got,
    block,
    block_got,
    every,
    every_modes,
    basis_high,
    basis_low,
    load_sem,
    send1,
    recv1,
    send2,
    recv2,
    send3,
    recv3,
    send4,
    recv4,
    send5,
    recv5,
    send6,
    recv6,
    send7,
    recv7,
):
    groups, cols, chunk, chunks, taps, comp, events, samples = sizes
    row, col = lax.axis_index("row"), lax.axis_index("col")
    group, place = row // GROUP, lax.rem(row, GROUP)
    width = refl.shape[1]

    def mate(o):
        return (group * GROUP + lax.rem(place + o, GROUP), col)

    def across(o):
        return (lax.rem(group + o, groups) * GROUP + place, col)

    def beside(o):
        return (row, lax.rem(col + o, cols))

    def send(src, dst, sems, where):
        return pltpu.make_async_remote_copy(
            src_ref=src,
            dst_ref=dst,
            send_sem=sems[0],
            recv_sem=sems[1],
            device_id=where,
            device_id_type=MESH,
        )

    def load(i, start):
        at = pl.ds(pl.multiple_of(i * chunk, chunk), chunk)
        for k, (src, dst) in enumerate(((refl_hbm, refl), (vec_hbm, vec))):
            copy = pltpu.make_async_copy(src.at[at], dst.at[at], load_sem.at[i, k])
            copy.start() if start else copy.wait()

    for i in range(chunks):
        load(i, True)
    barrier = pltpu.get_barrier_semaphore()
    others = (
        [mate(o) for o in range(1, GROUP)]
        + [across(o) for o in range(1, groups)]
        + [beside(o) for o in range(1, cols)]
    )
    for other in others:
        pl.semaphore_signal(barrier, inc=1, device_id=other, device_id_type=MESH)

    panel[...] = jnp.zeros_like(panel)

    @pl.loop(0, chunks)
    def _(i):
        load(i, False)
        at = pl.ds(pl.multiple_of(i * chunk, chunk), chunk)
        panel[...] += dot3(split(refl[at, :]), split(vec[at, :]), (0, 0))

    part[...] = panel[...].reshape(part.shape)
    pl.semaphore_wait(barrier, len(others))

    first = [
        [
            send(
                part.at[h, lax.rem(place + o, GROUP)],
                part_got.at[h, o - 1],
                (send1.at[h, o - 1], recv1.at[h, o - 1]),
                mate(o),
            )
            for o in range(1, GROUP)
        ]
        for h in range(PARTS)
    ]
    for copies in first:
        for copy in copies:
            copy.start()
    wave = [
        send(
            modes_ref,
            every_modes.at[col],
            (send7.at[o - 1], recv7.at[o - 1]),
            beside(o),
        )
        for o in range(1, cols)
    ]
    for copy in wave:
        copy.start()

    total = groups * GROUP * comp + events

    def gather(begin, end):
        @pl.loop(begin, end)
        def _(c8):
            for u in range(8):
                c = c8 * 8 + u
                a, b = None, None
                for j in range(taps):
                    at = taps_ref[c * taps + j]
                    scale = weights_ref[c * taps + j]
                    x = vec[pl.ds(at, 1), :] * scale
                    y = refl[pl.ds(at, 1), :] * scale
                    a = x if a is None else a + x
                    b = y if b is None else b + y
                picked[pl.ds(c, 1), :] = a
                picked_refl[pl.ds(c, 1), :] = b

    third = total // 8 // 3
    gather(0, third)
    second = []
    for h in range(PARTS):
        for copy in first[h]:
            copy.wait()
        value = part[h, place]
        for o in range(1, GROUP):
            value = value + part_got[h, o - 1]
        mine[h] = value
        second.append(
            [
                send(
                    mine.at[h],
                    mine_got.at[h, o - 1],
                    (send2.at[h, o - 1], recv2.at[h, o - 1]),
                    across(o),
                )
                for o in range(1, groups)
            ]
        )
        for copy in second[h]:
            copy.start()
    gather(third, 2 * third)
    back = []
    for h in range(PARTS):
        for copy in second[h]:
            copy.wait()
        value = mine[h]
        for o in range(1, groups):
            value = value + mine_got[h, o - 1]
        whole[h, place] = value
        back.append(
            [
                send(
                    whole.at[h, place],
                    whole.at[h, place],
                    (send3.at[h, o - 1], recv3.at[h, o - 1]),
                    mate(o),
                )
                for o in range(1, GROUP)
            ]
        )
        for copy in back[h]:
            copy.start()
    gather(2 * third, total // 8)
    for h in range(PARTS):
        for copy in back[h]:
            copy.wait()
    folded = dot3(split(factor_ref[...]), split(whole[...].reshape(panel.shape)), (1, 0))
    high, low = split(folded)
    high_ref[...] = high
    low_ref[...] = low

    source = picked[groups * GROUP * comp :, :] - dot3(
        split(picked_refl[groups * GROUP * comp :, :]), (high, low), (1, 0)
    )
    for g in range(groups):
        at = slice(g * GROUP * comp, (g + 1) * GROUP * comp)
        value = picked[at, :] - dot3(split(picked_refl[at, :]), (high, low), (1, 0))
        for q in range(GROUP):
            sums[q, g, :comp, :] = value[q * comp : (q + 1) * comp, :]
            sums[q, g, comp:, :] = source
    copies = [
        send(
            sums.at[lax.rem(place + o, GROUP)],
            sums_got.at[o - 1],
            (send4.at[o - 1], recv4.at[o - 1]),
            mate(o),
        )
        for o in range(1, GROUP)
    ]
    for copy in copies:
        copy.start()

    every_modes[col] = modes_ref[...]
    for copy in wave:
        copy.wait()
    step = min(samples, 32)
    for c in range(cols):
        freq, damp = every_modes[c, 0:1, :], every_modes[c, 1:2, :]

        @pl.loop(0, samples // step)
        def _(i):
            begin = pl.multiple_of(i * step, step)
            shape = (step, freq.shape[1])
            times = (lax.broadcasted_iota(jnp.int32, shape, 0) + (col * samples + begin)).astype(F32)
            value = jnp.exp(-damp * times) * cosine(freq * times)
            basis_high[c, pl.ds(begin, step), :], basis_low[c, pl.ds(begin, step), :] = split(value)

    for copy in copies:
        copy.wait()
    value = sums[place]
    for o in range(1, GROUP):
        value = value + sums_got[o - 1]
    block[...] = value
    copies = [
        send(
            block.at[lax.rem(group + o, groups)],
            block_got.at[o - 1],
            (send5.at[o - 1], recv5.at[o - 1]),
            across(o),
        )
        for o in range(1, groups)
    ]
    for copy in copies:
        copy.start()
    for copy in copies:
        copy.wait()
    value = block[group]
    for o in range(1, groups):
        value = value + block_got[o - 1]
    every[col] = value
    copies = [
        send(
            every.at[col],
            every.at[col],
            (send6.at[o - 1], recv6.at[o - 1]),
            beside(o),
        )
        for o in range(1, cols)
    ]
    for copy in copies:
        copy.start()
    for copy in copies:
        copy.wait()

    result = None
    for c in range(cols):
        receivers = every[c, :comp, :]
        amplitude = jnp.concatenate(
            [every[c, comp + e : comp + e + 1, :] * receivers for e in range(events)], axis=0
        )
        value = dot3(split(amplitude), (basis_high[c], basis_low[c]), (1, 1))
        result = value if result is None else result + value
    scale = 1.0 / float(cols * vec.shape[1]) ** 0.5
    seis_ref[...] = (result * scale).reshape(seis_ref.shape)


def update_kernel(vec_ref, refl_ref, high_ref, low_ref, out_ref):
    folded = (high_ref[...], low_ref[...])
    out_ref[...] = vec_ref[...] - dot3(split(refl_ref[...]), folded, (1, 0))


def shards(
    rows,
    cols,
    vectors,
    reflectors,
    panel_factor,
    station_rows,
    station_weights,
    event_rows,
    event_weights,
    mode_freq,
    mode_damp,
):
    here, wide = vectors.shape
    width = reflectors.shape[1]
    comps, taps = station_rows.shape
    events = event_rows.shape[0]
    comp = comps // rows
    samples = 1024 // cols
    groups = rows // GROUP
    chunk = min(1024, here)
    chunks = here // chunk

    local = jnp.concatenate([station_rows, event_rows]).reshape(-1) - lax.axis_index("row") * here
    weights = jnp.concatenate([station_weights, event_weights]).reshape(-1)
    weights = jnp.where((local >= 0) & (local < here), weights, 0.0)
    local = jnp.clip(local, 0, here - 1)
    modes = jnp.pad(jnp.stack([mode_freq, mode_damp]), ((0, 6), (0, 0)))

    piece = width // PARTS // GROUP
    tall = comp + events
    dma = pltpu.SemaphoreType.DMA
    out_groups, out_cols = max(groups - 1, 1), max(cols - 1, 1)
    in_vmem = pl.BlockSpec(memory_space=pltpu.VMEM)
    in_smem = pl.BlockSpec(memory_space=pltpu.SMEM)
    in_any = pl.BlockSpec(memory_space=pl.ANY)
    sizes = (groups, cols, chunk, chunks, taps, comp, events, samples)
    high, low, seismograms = pl.pallas_call(
        functools.partial(panel_kernel, sizes),
        out_shape=(
            jax.ShapeDtypeStruct((width, wide), BF16),
            jax.ShapeDtypeStruct((width, wide), BF16),
            jax.ShapeDtypeStruct((events, comp, samples), F32),
        ),
        in_specs=[in_smem, in_smem, in_any, in_any, in_vmem, in_vmem],
        out_specs=(in_vmem, in_vmem, in_vmem),
        scratch_shapes=[
            pltpu.VMEM((here, wide), F32),
            pltpu.VMEM((here, width), F32),
            pltpu.VMEM((PARTS, GROUP, piece, wide), F32),
            pltpu.VMEM((PARTS, GROUP - 1, piece, wide), F32),
            pltpu.VMEM((PARTS, piece, wide), F32),
            pltpu.VMEM((PARTS, out_groups, piece, wide), F32),
            pltpu.VMEM((width, wide), F32),
            pltpu.VMEM((PARTS, GROUP, piece, wide), F32),
            pltpu.VMEM((comps + events, wide), F32),
            pltpu.VMEM((comps + events, width), F32),
            pltpu.VMEM((GROUP, groups, tall, wide), F32),
            pltpu.VMEM((GROUP - 1, groups, tall, wide), F32),
            pltpu.VMEM((groups, tall, wide), F32),
            pltpu.VMEM((out_groups, tall, wide), F32),
            pltpu.VMEM((cols, tall, wide), F32),
            pltpu.VMEM((cols, 8, wide), F32),
            pltpu.VMEM((cols, samples, wide), BF16),
            pltpu.VMEM((cols, samples, wide), BF16),
            dma((chunks, 2)),
            dma((PARTS, GROUP - 1)),
            dma((PARTS, GROUP - 1)),
            dma((PARTS, out_groups)),
            dma((PARTS, out_groups)),
            dma((PARTS, GROUP - 1)),
            dma((PARTS, GROUP - 1)),
            dma((GROUP - 1,)),
            dma((GROUP - 1,)),
            dma((out_groups,)),
            dma((out_groups,)),
            dma((out_cols,)),
            dma((out_cols,)),
            dma((out_cols,)),
            dma((out_cols,)),
        ],
        compiler_params=pltpu.CompilerParams(
            collective_id=0, has_side_effects=True, vmem_limit_bytes=48 * 2**20
        ),
        cost_estimate=pl.CostEstimate(
            flops=6 * here * width * wide,
            bytes_accessed=4 * here * (wide + width),
            transcendentals=0,
        ),
    )(local, weights, vectors, reflectors, panel_factor, modes)

    tile = min(1024, here)
    rotated = pl.pallas_call(
        update_kernel,
        grid=(here // tile,),
        out_shape=jax.ShapeDtypeStruct((here, wide), F32),
        in_specs=[
            pl.BlockSpec((tile, wide), lambda i: (i, 0)),
            pl.BlockSpec((tile, width), lambda i: (i, 0)),
            pl.BlockSpec((width, wide), lambda i: (0, 0)),
            pl.BlockSpec((width, wide), lambda i: (0, 0)),
        ],
        out_specs=pl.BlockSpec((tile, wide), lambda i: (i, 0)),
        compiler_params=pltpu.CompilerParams(vmem_limit_bytes=32 * 2**20),
        cost_estimate=pl.CostEstimate(
            flops=6 * here * width * wide,
            bytes_accessed=4 * here * (2 * wide + width),
            transcendentals=0,
        ),
    )(vectors, reflectors, high, low)
    return (rotated, seismograms)


def solution(mesh):
    placed = (P("row", "col"), P("row", None), P(), P(), P(), P(), P(), P("col"), P("col"))
    return jax.shard_map(
        functools.partial(shards, mesh.shape["row"], mesh.shape["col"]),
        mesh=mesh,
        in_specs=placed,
        out_specs=(P("row", "col"), P(None, "row", "col")),
        check_vma=False,
    )
```

```python
import functools
import math

import jax
import jax.numpy as jnp
import numpy as np
from jax import lax
from jax.experimental import pallas as pl
from jax.experimental.pallas import tpu as pltpu
from jax.sharding import PartitionSpec as P

MESH = pl.DeviceIdType.MESH
F32 = jnp.float32
BF16 = jnp.bfloat16
GROUP = 4

TURN_A = 6.28125
TURN_B = float(np.round((2 * math.pi - TURN_A) * 2**20) / 2**20)
TURN_C = 2 * math.pi - TURN_A - TURN_B


def cos_series():
    square = np.linspace(0.0, (1.01 * math.pi) ** 2, 4001)
    fit = np.polynomial.Chebyshev.fit(square, np.cos(np.sqrt(square)), 7)
    return [float(c) for c in fit.convert(kind=np.polynomial.Polynomial).coef]


COS = cos_series()


def cosine(x):
    turns = jnp.floor(x * (0.5 / math.pi) + 0.5)
    rest = ((x - turns * TURN_A) - turns * TURN_B) - turns * TURN_C
    square = rest * rest
    total = jnp.full_like(square, COS[-1])
    for coefficient in COS[-2::-1]:
        total = total * square + coefficient
    return total


def split(x):
    high = x.astype(BF16)
    return high, (x - high.astype(F32)).astype(BF16)


def dot3(a, b, over):
    dims = (((over[0],), (over[1],)), ((), ()))
    dot = functools.partial(lax.dot_general, dimension_numbers=dims, preferred_element_type=F32)
    return dot(a[0], b[0]) + (dot(a[0], b[1]) + dot(a[1], b[0]))


def panel_kernel(
    sizes,
    taps_ref,
    weights_ref,
    vec_hbm,
    refl_hbm,
    factor_hbm,
    freq_hbm,
    damp_hbm,
    vec,
    seis_ref,
    refl,
    freq_row,
    damp_row,
    factor,
    modes_ref,
    high_ref,
    low_ref,
    part,
    part_got,
    mine,
    mine_got,
    panel,
    whole,
    picked,
    picked_refl,
    sums,
    sums_got,
    block,
    block_got,
    every,
    every_modes,
    basis_high,
    basis_low,
    load_sem,
    small_sem,
    send1,
    recv1,
    send2,
    recv2,
    send3,
    recv3,
    send4,
    recv4,
    send5,
    recv5,
    send6,
    recv6,
    send7,
    recv7,
):
    parts, groups, cols, chunk, chunks, taps, comp, events, samples = sizes
    row, col = lax.axis_index("row"), lax.axis_index("col")
    group, place = row // GROUP, lax.rem(row, GROUP)
    width = refl.shape[1]

    def mate(o):
        return (group * GROUP + lax.rem(place + o, GROUP), col)

    def across(o):
        return (lax.rem(group + o, groups) * GROUP + place, col)

    def beside(o):
        return (row, lax.rem(col + o, cols))

    def send(src, dst, sems, where):
        return pltpu.make_async_remote_copy(
            src_ref=src,
            dst_ref=dst,
            send_sem=sems[0],
            recv_sem=sems[1],
            device_id=where,
            device_id_type=MESH,
        )

    lanes = vec.shape[1] // parts

    def loads(h, i):
        at = pl.ds(pl.multiple_of(i * chunk, chunk), chunk)
        here = pl.ds(h * lanes, lanes)
        found = [pltpu.make_async_copy(vec_hbm.at[at, here], vec.at[at, here], load_sem.at[i, h])]
        if h == 0:
            found.append(pltpu.make_async_copy(refl_hbm.at[at], refl.at[at], load_sem.at[i, parts]))
        return found

    for h in range(parts):
        for i in range(chunks):
            for copy in loads(h, i):
                copy.start()
    small = [
        pltpu.make_async_copy(src, dst, small_sem.at[k])
        for k, (src, dst) in enumerate(
            ((factor_hbm, factor), (freq_hbm, freq_row), (damp_hbm, damp_row))
        )
    ]
    for copy in small:
        copy.start()
    barrier = pltpu.get_barrier_semaphore()
    others = (
        [mate(o) for o in range(1, GROUP)]
        + [across(o) for o in range(1, groups)]
        + [beside(o) for o in range(1, cols)]
    )
    for other in others:
        pl.semaphore_signal(barrier, inc=1, device_id=other, device_id_type=MESH)

    first = []
    for h in range(parts):
        panel[...] = jnp.zeros_like(panel)

        @pl.loop(0, chunks)
        def _(i):
            for copy in loads(h, i):
                copy.wait()
            at = pl.ds(pl.multiple_of(i * chunk, chunk), chunk)
            here = slice(h * lanes, (h + 1) * lanes)
            panel[...] += dot3(split(refl[at, :]), split(vec[at, here]), (0, 0))

        part[h] = panel[...].reshape(part.shape[1:])
        if h == 0:
            pl.semaphore_wait(barrier, len(others))
        first.append(
            [
                send(
                    part.at[h, lax.rem(place + o, GROUP)],
                    part_got.at[h, o - 1],
                    (send1.at[h, o - 1], recv1.at[h, o - 1]),
                    mate(o),
                )
                for o in range(1, GROUP)
            ]
        )
        for copy in first[h]:
            copy.start()
    for copy in small:
        copy.wait()
    modes_ref[...] = jnp.zeros_like(modes_ref)
    modes_ref[0:1, :] = freq_row[...]
    modes_ref[1:2, :] = damp_row[...]
    wave = [
        send(
            modes_ref,
            every_modes.at[col],
            (send7.at[o - 1], recv7.at[o - 1]),
            beside(o),
        )
        for o in range(1, cols)
    ]
    for copy in wave:
        copy.start()

    total = groups * GROUP * comp + events

    def gather(begin, end):
        @pl.loop(begin, end)
        def _(c8):
            for u in range(8):
                c = c8 * 8 + u
                a, b = None, None
                for j in range(taps):
                    at = taps_ref[c * taps + j]
                    scale = weights_ref[c * taps + j]
                    x = vec[pl.ds(at, 1), :] * scale
                    y = refl[pl.ds(at, 1), :] * scale
                    a = x if a is None else a + x
                    b = y if b is None else b + y
                picked[pl.ds(c, 1), :] = a
                picked_refl[pl.ds(c, 1), :] = b

    third = total // 8 // 3
    gather(0, third)
    second = []
    for h in range(parts):
        for copy in first[h]:
            copy.wait()
        value = part[h, place]
        for o in range(1, GROUP):
            value = value + part_got[h, o - 1]
        mine[h] = value
        second.append(
            [
                send(
                    mine.at[h],
                    mine_got.at[h, o - 1],
                    (send2.at[h, o - 1], recv2.at[h, o - 1]),
                    across(o),
                )
                for o in range(1, groups)
            ]
        )
        for copy in second[h]:
            copy.start()
    gather(third, 2 * third)
    back = []
    for h in range(parts):
        for copy in second[h]:
            copy.wait()
        value = mine[h]
        for o in range(1, groups):
            value = value + mine_got[h, o - 1]
        whole[h, place] = value
        back.append(
            [
                send(
                    whole.at[h, place],
                    whole.at[h, place],
                    (send3.at[h, o - 1], recv3.at[h, o - 1]),
                    mate(o),
                )
                for o in range(1, GROUP)
            ]
        )
        for copy in back[h]:
            copy.start()
    gather(2 * third, total // 8)
    for h in range(parts):
        for copy in back[h]:
            copy.wait()
    upper = split(factor[...])
    for h in range(parts):
        here = slice(h * lanes, (h + 1) * lanes)
        folded = dot3(upper, split(whole[h].reshape(panel.shape)), (1, 0))
        high_ref[:, here], low_ref[:, here] = split(folded)
    high, low = high_ref[...], low_ref[...]

    source = picked[groups * GROUP * comp :, :] - dot3(
        split(picked_refl[groups * GROUP * comp :, :]), (high, low), (1, 0)
    )
    for g in range(groups):
        at = slice(g * GROUP * comp, (g + 1) * GROUP * comp)
        value = picked[at, :] - dot3(split(picked_refl[at, :]), (high, low), (1, 0))
        for q in range(GROUP):
            sums[q, g, :events, :] = source
            sums[q, g, events:, :] = value[q * comp : (q + 1) * comp, :]
    spans = ((0, events + comp // 2), (events + comp // 2, comp - comp // 2))
    within = []
    for h, (low_row, tall) in enumerate(spans):
        at = pl.ds(low_row, tall)
        within.append(
            [
                send(
                    sums.at[lax.rem(place + o, GROUP), :, at],
                    sums_got.at[o - 1, :, at],
                    (send4.at[h, o - 1], recv4.at[h, o - 1]),
                    mate(o),
                )
                for o in range(1, GROUP)
            ]
        )
        for copy in within[h]:
            copy.start()

    def update(begin, end):
        @pl.loop(begin, end)
        def _(i):
            at = pl.ds(pl.multiple_of(i * chunk, chunk), chunk)
            vec[at, :] = vec[at, :] - dot3(split(refl[at, :]), (high_ref[...], low_ref[...]), (1, 0))

    every_modes[col] = modes_ref[...]
    for copy in wave:
        copy.wait()
    update(0, chunks // 2)
    step = min(samples, 32)
    for c in range(cols):
        freq, damp = every_modes[c, 0:1, :], every_modes[c, 1:2, :]

        @pl.loop(0, samples // step)
        def _(i):
            begin = pl.multiple_of(i * step, step)
            shape = (step, freq.shape[1])
            times = (lax.broadcasted_iota(jnp.int32, shape, 0) + (col * samples + begin)).astype(F32)
            value = jnp.exp(-damp * times) * cosine(freq * times)
            basis_high[c, pl.ds(begin, step), :], basis_low[c, pl.ds(begin, step), :] = split(value)

    over = []
    for h, (low_row, tall) in enumerate(spans):
        at = pl.ds(low_row, tall)
        for copy in within[h]:
            copy.wait()
        value = sums[place, :, at]
        for o in range(1, GROUP):
            value = value + sums_got[o - 1, :, at]
        block[:, at] = value
        over.append(
            [
                send(
                    block.at[lax.rem(group + o, groups), at],
                    block_got.at[o - 1, at],
                    (send5.at[h, o - 1], recv5.at[h, o - 1]),
                    across(o),
                )
                for o in range(1, groups)
            ]
        )
        for copy in over[h]:
            copy.start()
        if h == 0:
            update(chunks // 2, chunks * 3 // 4)
    update(chunks * 3 // 4, chunks)
    twin = (row, col + 1 - 2 * lax.rem(col, 2))
    pairs = cols // 2

    def carry(h, slot, whose, where):
        ref = every.at[whose, pl.ds(*spans[h])]
        return send(ref, ref, (send6.at[h, slot], recv6.at[h, slot]), where)

    near, far, passed = [], [], []
    for h, (low_row, tall) in enumerate(spans):
        at = pl.ds(low_row, tall)
        for copy in over[h]:
            copy.wait()
        value = block[group, at]
        for o in range(1, groups):
            value = value + block_got[o - 1, at]
        every[col, at] = value
        far.append([carry(h, o - 1, col, beside(2 * o)) for o in range(1, pairs)])
        near.append(carry(h, pairs - 1, col, twin))
        for copy in far[h]:
            copy.start()
        near[h].start()
    for h in range(2):
        for o in range(1, pairs):
            far[h][o - 1].wait()
            copy = carry(h, pairs - 1 + o, lax.rem(col - 2 * o + cols, cols), twin)
            copy.start()
            passed.append(copy)
    for copy in near + passed:
        copy.wait()

    result = None
    for c in range(cols):
        receivers = every[c, events:, :]
        amplitude = jnp.concatenate(
            [every[c, e : e + 1, :] * receivers for e in range(events)], axis=0
        )
        value = dot3(split(amplitude), (basis_high[c], basis_low[c]), (1, 1))
        result = value if result is None else result + value
    scale = 1.0 / float(cols * vec.shape[1]) ** 0.5
    seis_ref[...] = (result * scale).reshape(seis_ref.shape)


def shards(
    rows,
    cols,
    vectors,
    reflectors,
    panel_factor,
    station_rows,
    station_weights,
    event_rows,
    event_weights,
    mode_freq,
    mode_damp,
):
    here, wide = vectors.shape
    width = reflectors.shape[1]
    comps, taps = station_rows.shape
    events = event_rows.shape[0]
    comp = comps // rows
    samples = 1024 // cols
    groups = rows // GROUP
    chunk = min(1024, here)
    chunks = here // chunk

    local = jnp.concatenate([station_rows, event_rows]).reshape(-1) - lax.axis_index("row") * here
    weights = jnp.concatenate([station_weights, event_weights]).reshape(-1)
    weights = jnp.where((local >= 0) & (local < here), weights, 0.0)
    local = jnp.clip(local, 0, here - 1)

    parts = 2 if wide % 256 == 0 else 1
    lanes = wide // parts
    piece = width // GROUP
    tall = comp + events
    dma = pltpu.SemaphoreType.DMA
    out_groups, out_cols = max(groups - 1, 1), max(cols - 1, 1)
    in_vmem = pl.BlockSpec(memory_space=pltpu.VMEM)
    in_smem = pl.BlockSpec(memory_space=pltpu.SMEM)
    in_hbm = pl.BlockSpec(memory_space=pltpu.HBM)
    sizes = (parts, groups, cols, chunk, chunks, taps, comp, events, samples)
    rotated, seismograms = pl.pallas_call(
        functools.partial(panel_kernel, sizes),
        out_shape=(
            pltpu.VMEM((here, wide), F32),
            jax.ShapeDtypeStruct((events, comp, samples), F32),
        ),
        in_specs=[in_smem, in_smem, in_hbm, in_hbm, in_hbm, in_hbm, in_hbm],
        out_specs=(in_vmem, in_vmem),
        scratch_shapes=[
            pltpu.VMEM((here, width), F32),
            pltpu.VMEM((1, wide), F32),
            pltpu.VMEM((1, wide), F32),
            pltpu.VMEM((width, width), F32),
            pltpu.VMEM((8, wide), F32),
            pltpu.VMEM((width, wide), BF16),
            pltpu.VMEM((width, wide), BF16),
            pltpu.VMEM((parts, GROUP, piece, lanes), F32),
            pltpu.VMEM((parts, GROUP - 1, piece, lanes), F32),
            pltpu.VMEM((parts, piece, lanes), F32),
            pltpu.VMEM((parts, out_groups, piece, lanes), F32),
            pltpu.VMEM((width, lanes), F32),
            pltpu.VMEM((parts, GROUP, piece, lanes), F32),
            pltpu.VMEM((comps + events, wide), F32),
            pltpu.VMEM((comps + events, width), F32),
            pltpu.VMEM((GROUP, groups, tall, wide), F32),
            pltpu.VMEM((GROUP - 1, groups, tall, wide), F32),
            pltpu.VMEM((groups, tall, wide), F32),
            pltpu.VMEM((out_groups, tall, wide), F32),
            pltpu.VMEM((cols, tall, wide), F32),
            pltpu.VMEM((cols, 8, wide), F32),
            pltpu.VMEM((cols, samples, wide), BF16),
            pltpu.VMEM((cols, samples, wide), BF16),
            dma((chunks, parts + 1)),
            dma((3,)),
            dma((parts, GROUP - 1)),
            dma((parts, GROUP - 1)),
            dma((parts, out_groups)),
            dma((parts, out_groups)),
            dma((parts, GROUP - 1)),
            dma((parts, GROUP - 1)),
            dma((2, GROUP - 1)),
            dma((2, GROUP - 1)),
            dma((2, out_groups)),
            dma((2, out_groups)),
            dma((2, out_cols)),
            dma((2, out_cols)),
            dma((out_cols,)),
            dma((out_cols,)),
        ],
        compiler_params=pltpu.CompilerParams(
            collective_id=0, has_side_effects=True, vmem_limit_bytes=30 * 2**20
        ),
        cost_estimate=pl.CostEstimate(
            flops=12 * here * width * wide,
            bytes_accessed=4 * here * (wide + width),
            transcendentals=0,
        ),
    )(
        local,
        weights,
        vectors,
        reflectors,
        pltpu.with_memory_space_constraint(panel_factor, pltpu.HBM),
        pltpu.with_memory_space_constraint(mode_freq.reshape(1, wide), pltpu.HBM),
        pltpu.with_memory_space_constraint(mode_damp.reshape(1, wide), pltpu.HBM),
    )
    return (rotated, seismograms)


def solution(mesh):
    placed = (P("row", "col"), P("row", None), P(), P(), P(), P(), P(), P("col"), P("col"))
    return jax.shard_map(
        functools.partial(shards, mesh.shape["row"], mesh.shape["col"]),
        mesh=mesh,
        in_specs=placed,
        out_specs=(P("row", "col"), P(None, "row", "col")),
        check_vma=False,
    )
```
